32 devices in a mesh: row: 4 (over y, core), col: 8 (over z, x).
Axes of the slice: x: 2, y: 2, z: 4, core: 2. Of those that a mesh axis runs over, the one named last changes fastest.
Arguments:
- grad_out: bfloat16 [2048, 8192], P('col', 'row'), may hold values from -0.09375 to 0.09375
- activations: bfloat16 [2048, 28672], P('row', 'col'), may hold values from -6 to 6
- left_steps: float32 [10, 8192], P(None, 'row')
- left_curves: float32 [10, 8192], P(None, 'row'), as said below
- right_steps: float32 [10, 28672], P(None, 'col')
- right_curves: float32 [10, 28672], P(None, 'col'), as said below
Outputs:
- direction: float32 [8192, 28672], P('row', 'col')
The draws below stay inside these ranges and needn't reach their ends.
Inputs may be any that keep to these rules, and one draw needn't show every extreme that they name: `left_curves`: each curve row is its step row scaled entrywise by positive factors, so every step has a positive inner product with its curve; the last pair is the newest. `right_curves`: as for the output side.
All inputs are finite; a program needn't handle non-finite values.
Results may differ from the reference program's by a relative error of at most 0.0003.
Values may be sent and summed in bfloat16 or wider, within the bound.
A program may use at most 192 MiB of HBM per device.

```python
import math
import jax
import jax.numpy as jnp
from jax import lax

D = 8192
FF = 28672
TOKENS = 2048
PAIRS = 10


def history(key, width, salt):
    base = jax.random.fold_in(key, salt)
    first, second, third, fourth = jax.random.split(base, 4)
    step_rows = jax.random.normal(first, (PAIRS, width), jnp.float32)
    curvature = jnp.exp(jax.random.uniform(second, (PAIRS, 1), jnp.float32, math.log(0.03), 0.0))
    newest = jax.random.uniform(fourth, (PAIRS, 1), jnp.float32, 0.5, 1.0)
    position = jnp.arange(PAIRS).reshape(PAIRS, 1)
    curvature = jnp.where(position == PAIRS - 1, newest, curvature)
    wobble = jax.random.uniform(third, (PAIRS, width), jnp.float32, -1.0, 1.0)
    return (step_rows, curvature * step_rows * (1.0 + 0.5 * wobble))


def draw_left_steps(key, part):
    return history(key, D, 7)[0]


def draw_left_curves(key, part):
    return history(key, D, 7)[1]


def draw_right_steps(key, part):
    return history(key, FF, 11)[0]


def draw_right_curves(key, part):
    return history(key, FF, 11)[1]


def shard_levels(key, dims, pieces, least, largest):
    gain = 1.0
    for dim, blocks in pieces:
        draws = jax.random.uniform(jax.random.fold_in(jax.random.fold_in(key, 6), dim), (blocks,), jnp.float32, least / len(pieces), largest / len(pieces))
        gain = gain * jnp.repeat(jnp.exp(draws), dims[dim] // blocks).reshape((-1,) + (1,) * (len(dims) - 1 - dim))
    return gain


def noise(rng, shape, scale, most, cuts=(), kind=jnp.bfloat16):
    drawn = scale * jax.random.normal(rng, shape, jnp.float32)
    if cuts:
        drawn = drawn * shard_levels(rng, shape, cuts, -0.22, 0.18)
    return jnp.clip(drawn, -most, most).astype(kind)


def setup_inputs(seed: int = 0) -> dict:
    seeds = jax.random.split(jax.random.key(seed), 7)
    grad_out = noise(seeds[0], (TOKENS, D), 0.015625, 0.09375, ((0, 8), (1, 4)))
    activations = noise(seeds[1], (TOKENS, FF), 1.0, 6.0, ((0, 4), (1, 8)))
    left_steps = draw_left_steps(jax.random.fold_in(seeds[6], 71), 0)
    left_curves = draw_left_curves(jax.random.fold_in(seeds[6], 71), 0)
    right_steps = draw_right_steps(jax.random.fold_in(seeds[6], 71), 0)
    right_curves = draw_right_curves(jax.random.fold_in(seeds[6], 71), 0)
    return dict(grad_out=grad_out, activations=activations, left_steps=left_steps, left_curves=left_curves, right_steps=right_steps, right_curves=right_curves)


HIGH = lax.Precision.HIGHEST


def side_terms(step_rows, curv_rows):
    pair_sy = jnp.dot(step_rows, curv_rows.T, precision=HIGH, preferred_element_type=jnp.float32)
    pair_yy = jnp.dot(curv_rows, curv_rows.T, precision=HIGH, preferred_element_type=jnp.float32)
    return pair_sy, pair_yy


def upper_inverse(upper_tri):
    count = upper_tri.shape[0]
    identity = jnp.eye(count, dtype=upper_tri.dtype)
    inv_rows = [None] * count
    for index in reversed(range(count)):
        running = identity[index]
        for later in range(index + 1, count):
            running = running - upper_tri[index, later] * inv_rows[later]
        inv_rows[index] = running / upper_tri[index, index]
    return jnp.stack(inv_rows, 0)


def compact(pair_sy, pair_yy):
    scaling = pair_sy[-1, -1] / pair_yy[-1, -1]
    upper_tri = jnp.triu(pair_sy)
    inverse = upper_inverse(upper_tri)
    middle = jnp.diag(jnp.diag(pair_sy)) + scaling * pair_yy
    return scaling, inverse, middle


def reference(grad_out, activations, left_steps, left_curves, right_steps, right_curves):
    grad = lax.dot_general(grad_out, activations, (((0,), (0,)), ((), ())), preferred_element_type=jnp.float32)
    l_scale, l_inv, l_mid = compact(*side_terms(left_steps, left_curves))
    r_scale, r_inv, r_mid = compact(*side_terms(right_steps, right_curves))
    proj_steps = jnp.dot(left_steps, grad, precision=HIGH)
    proj_curves = jnp.dot(left_curves, grad, precision=HIGH)
    weighted = jnp.dot(l_inv, proj_steps, precision=HIGH)
    coeffs = jnp.dot(l_inv.T, jnp.dot(l_mid, weighted, precision=HIGH) - l_scale * proj_curves, precision=HIGH)
    lefted = l_scale * grad + jnp.dot(left_steps.T, coeffs, precision=HIGH) - l_scale * jnp.dot(left_curves.T, weighted, precision=HIGH)
    side_steps = jnp.dot(lefted, right_steps.T, precision=HIGH)
    side_curves = jnp.dot(lefted, right_curves.T, precision=HIGH)
    rweighted = jnp.dot(side_steps, r_inv.T, precision=HIGH)
    rcoeffs = jnp.dot(jnp.dot(rweighted, r_mid, precision=HIGH) - r_scale * side_curves, r_inv, precision=HIGH)
    return r_scale * lefted + jnp.dot(rcoeffs, right_steps, precision=HIGH) - r_scale * jnp.dot(rweighted, right_curves, precision=HIGH)
```

```python
import functools
import jax
import jax.numpy as jnp
from jax import lax
from jax.experimental import pallas as pl
from jax.experimental.pallas import tpu as pltpu
from jax.sharding import PartitionSpec as P

HIGH = lax.Precision.HIGHEST
MESH = pl.DeviceIdType.MESH
F32, BF16 = jnp.float32, jnp.bfloat16
HALF = 16
BOTH = 2 * HALF


def dot(a, b, ca, cb):
    return lax.dot_general(a, b, (((ca,), (cb,)), ((), ())), precision=HIGH, preferred_element_type=F32)


def bdot(a, b, ca, cb):
    return lax.dot_general(a, b, (((ca,), (cb,)), ((), ())), preferred_element_type=F32)


def pieces(x, count):
    out = []
    for _ in range(count):
        top = x.astype(BF16).astype(F32)
        out.append(top)
        x = x - top
    return out


def times_pieces(x, mat):
    rows = x.shape[0]
    got = bdot(jnp.concatenate(pieces(x, 3), 0).astype(BF16), mat, 1, 1)
    return got[:rows] + got[rows : 2 * rows] + got[2 * rows :]


def compact(prod, pairs):
    sub = lax.broadcasted_iota(jnp.int32, (HALF, HALF), 0)
    lane = lax.broadcasted_iota(jnp.int32, (HALF, HALF), 1)
    sy, yy = prod[:HALF], prod[HALF:]

    def pick(x, mask, axes):
        x = jnp.where(mask, x, 0.0)
        for axis in axes:
            x = jnp.sum(x, axis=axis, keepdims=True)
        return x

    last = (sub == pairs - 1) & (lane == pairs - 1)
    scaling = pick(sy, last, (0, 1)) / pick(yy, last, (0, 1))
    upper = jnp.where(sub <= lane, sy, 0.0)
    inv = jnp.where((sub == lane) & (sub < pairs), 1.0, 0.0)
    for j in reversed(range(pairs)):
        column = pick(upper, lane == j, (1,))
        row = pick(inv, sub == j, (0,)) / pick(upper, (sub == j) & (lane == j), (0, 1))
        inv = jnp.where(sub == j, row, jnp.where(sub < j, inv - column * row, inv))
    middle = jnp.where(sub == lane, sy, 0.0) + scaling * yy
    return scaling, inv, middle


def apply_terms(terms, x):
    scaling, inv, middle = terms
    weighted = dot(inv, x[:HALF], 1, 0)
    coeffs = dot(inv, dot(middle, weighted, 1, 0) - scaling * x[HALF:], 0, 0)
    return jnp.concatenate([coeffs, -scaling * weighted], 0)


def stages(n):
    return n.bit_length() - 1


def gather_kernel(
    nrow, ncol, pairs, aligned, cuts, spread,
    act, go, lpair, rpair,
    act_full, gt_full, lf_out, rf_out, x2_out, s_out,
    gt, act_v, l_msg, r_msg, l_in, r_in, l_sum, r_sum, l_all, r_all, l_cat, r_cat,
    local_sem, cw_s, cw_r, cc_s, cc_r, y_s, y_r, sib_s, sib_r,
    l1_s, l1_r, r1_s, r1_r, l2_s, l2_r, r2_s, r2_r,
):
    r, c = lax.axis_index("row"), lax.axis_index("col")
    tok_r, tok_c, dloc = act.shape[0], go.shape[0], go.shape[1]
    ny = nrow // 2
    y, core = r // 2, r % 2
    nz = ncol // 2

    def dev(row, col):
        return {"row": row, "col": col}

    barrier = pltpu.get_barrier_semaphore()
    for d in range(1, nrow):
        pl.semaphore_signal(barrier, inc=1, device_id=dev((r + d) % nrow, c), device_id_type=MESH)
    for d in range(1, ncol):
        pl.semaphore_signal(barrier, inc=1, device_id=dev(r, (c + d) % ncol), device_id_type=MESH)
    pl.semaphore_wait(barrier, nrow + ncol - 2)

    pending = []

    def remote(src, dst, send, recv, row, col):
        copy = pltpu.make_async_remote_copy(
            src_ref=src, dst_ref=dst, send_sem=send, recv_sem=recv,
            device_id=dev(row, col), device_id_type=MESH)
        copy.start()
        pending.append(copy)
        return copy

    def local(src, dst, sem):
        copy = pltpu.make_async_copy(src, dst, sem)
        copy.start()
        return copy

    step_a = tok_r // (2 * cuts)

    def act_at(row, part):
        start = row * tok_r + part * step_a
        return act_full.at[pl.ds(pl.multiple_of(start, 16), step_a), :]

    def y_parts(k, way):
        full = ny // 2 - 1
        mine = range(way * cuts, (way + 1) * cuts)
        other = range((1 - way) * cuts, (2 - way) * cuts)
        return list(mine) + (list(other) if k < full else [])

    def y_send(k, way, part):
        sign = 1 - 2 * way
        origin = ((y - sign * k + ny) % ny) * 2 + core
        target = ((y + sign + ny) % ny) * 2 + core
        src = act.at[pl.ds(part * step_a, step_a), :] if k == 0 else act_at(origin, part)
        idx = (way, k, part)
        remote(src, act_at(origin, part), y_s.at[idx], y_r.at[idx], target, c)

    def y_wait(k, way, part):
        sign = 1 - 2 * way
        origin = ((y - sign * (k + 1) + 2 * ny) % ny) * 2 + core
        piece = act_at(origin, part)
        idx = (way, k, part)
        pltpu.make_async_remote_copy(
            src_ref=piece, dst_ref=piece, send_sem=y_s.at[idx], recv_sem=y_r.at[idx],
            device_id=dev(r, c), device_id_type=MESH).wait_recv()
        remote(piece, piece, sib_s.at[idx], sib_r.at[idx], y * 2 + 1 - core, c)
        if k + 1 < max(ny // 2, 1) and part in y_parts(k + 1, way):
            y_send(k + 1, way, part)

    for part in range(cuts):
        y_send(0, 0, part)
        y_send(0, 1, cuts + part)
    if ny > 2:
        for part in range(cuts):
            y_send(0, 0, cuts + part)
            y_send(0, 1, part)
    own_act = act_full.at[pl.ds(pl.multiple_of(r * tok_r, 16), tok_r), :]
    own_sib = pltpu.make_async_remote_copy(
        src_ref=act, dst_ref=own_act, send_sem=local_sem.at[3], recv_sem=local_sem.at[4],
        device_id=dev(y * 2 + 1 - core, c), device_id_type=MESH)
    own_sib.start()
    to_v = local(act, act_v, local_sem.at[0])
    keep_act = local(act, own_act, local_sem.at[1])

    for i in range(dloc // 128):
        rows = slice(i * 128, (i + 1) * 128)
        gt[rows, :] = go[:, rows].astype(F32).T.astype(BF16)
    half = dloc // 2
    zc, xc = c // 2, c % 2
    pos = (1 - xc) * zc + xc * (ncol - 1 - zc)

    def col_of(p):
        x = p // nz
        return ((1 - x) * p + x * (ncol - 1 - p)) * 2 + x

    def gt_at(col, h):
        if aligned:
            return gt_full.at[pl.ds(h * half, half), pl.ds(pl.multiple_of(col * tok_c, 128), tok_c)]
        return gt_full.at[col, pl.ds(h * half, half), :]

    def ring_halves(k, way):
        return [way, 1 - way] if k < ncol // 2 - 1 else [way]

    def ring_send(k, way, h):
        sign = 1 - 2 * way
        origin = col_of((pos - sign * k + ncol) % ncol)
        target = col_of((pos + sign + ncol) % ncol)
        src = gt.at[pl.ds(h * half, half), :] if k == 0 else gt_at(origin, h)
        send, recv = (cc_s, cc_r) if way else (cw_s, cw_r)
        remote(src, gt_at(origin, h), send.at[k, h], recv.at[k, h], r, target)

    def ring_wait(k, way, h):
        sign = 1 - 2 * way
        origin = col_of((pos - sign * (k + 1) + ncol) % ncol)
        piece = gt_at(origin, h)
        send, recv = (cc_s, cc_r) if way else (cw_s, cw_r)
        pltpu.make_async_remote_copy(
            src_ref=piece, dst_ref=piece, send_sem=send.at[k, h], recv_sem=recv.at[k, h],
            device_id=dev(r, c), device_id_type=MESH).wait_recv()
        if k + 1 < ncol // 2 and h in ring_halves(k + 1, way):
            ring_send(k + 1, way, h)

    for i in range(2):
        for way in range(2):
            ring_send(0, way, ring_halves(0, way)[i])
    if aligned:
        own_gt = gt_full.at[:, pl.ds(pl.multiple_of(c * tok_c, 128), tok_c)]
    else:
        own_gt = gt_full.at[c]
    keep_gt = local(gt, own_gt, local_sem.at[2])

    def first_part():
        lanes_l, lanes_r = l_msg.shape[1] - 128, r_msg.shape[1] - 128
        l_msg[...] = jnp.zeros_like(l_msg)
        l_msg[:, :tok_c] = times_pieces(lpair[...], go[...])
        l_msg[:, lanes_l : lanes_l + HALF] = dot(lpair[...], lpair[HALF:, :], 1, 1)
        to_v.wait()
        r_msg[...] = jnp.zeros_like(r_msg)
        r_msg[:, :tok_r] = times_pieces(rpair[...], act_v[...])
        r_msg[:, lanes_r : lanes_r + HALF] = dot(rpair[...], rpair[HALF:, :], 1, 1)
        l_sum[0] = l_msg[...]
        r_sum[0] = r_msg[...]

    def partner(i, s):
        return i + (1 - 2 * ((i // 2**s) % 2)) * 2**s

    def sum_start(s):
        if s < stages(nrow):
            remote(l_sum.at[s], l_in.at[s], l1_s.at[s], l1_r.at[s], partner(r, s), c)
        if s < stages(ncol):
            remote(r_sum.at[s], r_in.at[s], r1_s.at[s], r1_r.at[s], r, partner(c, s))

    def arrived(ref, send, recv):
        pltpu.make_async_remote_copy(
            src_ref=ref, dst_ref=ref, send_sem=send, recv_sem=recv,
            device_id=dev(r, c), device_id_type=MESH).wait_recv()

    def sum_end(s):
        if s < stages(nrow):
            arrived(l_in.at[s], l1_s.at[s], l1_r.at[s])
            l_sum[s + 1] = l_sum[s] + l_in[s]
        if s < stages(ncol):
            arrived(r_in.at[s], r1_s.at[s], r1_r.at[s])
            r_sum[s + 1] = r_sum[s] + r_in[s]

    ls, rs = stages(nrow), stages(ncol)

    def spread_sums():
        l_own = l_sum.at[ls, :, pl.ds(0, l_all.shape[2])]
        r_own = r_sum.at[rs, :, pl.ds(0, r_all.shape[2])]
        for d in range(1, ncol):
            remote(l_own, l_all.at[c], l2_s.at[d], l2_r.at[d], r, (c + d) % ncol)
        for d in range(1, nrow):
            remote(r_own, r_all.at[r], r2_s.at[d], r2_r.at[d], (r + d) % nrow, c)
        l_all[c] = l_sum[ls, :, : l_all.shape[2]]
        r_all[r] = r_sum[rs, :, : r_all.shape[2]]

    def last_part():
        for d in range(1, ncol):
            arrived(l_all.at[(c + ncol - d) % ncol], l2_s.at[d], l2_r.at[d])
        for d in range(1, nrow):
            arrived(r_all.at[(r + nrow - d) % nrow], r2_s.at[d], r2_r.at[d])
        for i in range(ncol):
            l_cat[:, i * tok_c : (i + 1) * tok_c] = l_all[i, :, :tok_c]
        for i in range(nrow):
            r_cat[:, i * tok_r : (i + 1) * tok_r] = r_all[i, :, :tok_r]
        left = compact(l_sum[ls, :, l_all.shape[2] : l_all.shape[2] + HALF], pairs)
        right = compact(r_sum[rs, :, r_all.shape[2] : r_all.shape[2] + HALF], pairs)
        lf = right[0] * apply_terms(left, l_cat[...])
        rf = left[0] * apply_terms(right, r_cat[...])
        for i, piece in enumerate(pieces(lf, 3)):
            lf_out[i * BOTH : (i + 1) * BOTH, :] = piece.astype(BF16)
        for i, piece in enumerate(pieces(rf, 3)):
            rf_out[i * BOTH : (i + 1) * BOTH, :] = piece.astype(BF16)
        cross = dot(l_cat[...], r_cat[...], 1, 1)
        x2_out[...] = apply_terms(right, dot(cross, apply_terms(left, lpair[...]), 0, 0))
        s_out[...] = jnp.broadcast_to(left[0] * right[0], s_out.shape)

    todo = []
    ring_total = ncol - 1
    for k in range(ncol // 2):
        for i, _ in enumerate(ring_halves(k, 0)):
            for way in range(2):
                h = ring_halves(k, way)[i]
                todo.append(((2 * k + i + 1) / ring_total, functools.partial(ring_wait, k, way, h)))
    y_count = sum(len(y_parts(k, 0)) for k in range(max(ny // 2, 1)))
    done = 0
    for k in range(max(ny // 2, 1)):
        for i in range(len(y_parts(k, 0))):
            done += 1
            for way in range(2):
                todo.append((done / y_count, functools.partial(y_wait, k, way, y_parts(k, way)[i])))
    small = [first_part, functools.partial(sum_start, 0)]
    for s in range(max(ls, rs)):
        small.append((lambda s: lambda: (sum_end(s), sum_start(s + 1)))(s))
    small += [spread_sums, last_part]
    for i, f in enumerate(small):
        todo.append((max(0, i - 1) * spread + 0.001, f))
    todo.sort(key=lambda item: item[0])
    for _, f in todo:
        f()
    own_sib.wait()
    for k in range(max(ny // 2, 1)):
        for way in range(2):
            sign = 1 - 2 * way
            origin = ((y - sign * (k + 1) + 2 * ny) % ny) * 2 + 1 - core
            for part in y_parts(k, way):
                arrived(act_at(origin, part), sib_s.at[way, k, part], sib_r.at[way, k, part])
    keep_act.wait()
    keep_gt.wait()
    for copy in pending:
        copy.wait_send()


def apply_kernel(step_m, s_ref, gt, act, lf, rf, x2, lpair, rpair, out, a_ext, b_ext):
    wide = 2 * BOTH
    dloc = gt.shape[0]

    @pl.when(pl.program_id(0) == 0)
    def _():
        got = bdot(rf[...], gt[...], 1, 1)
        second = got[:BOTH] + got[BOTH : 2 * BOTH] + got[2 * BOTH :] + x2[...]
        hi, lo = pieces(jnp.concatenate([lpair[...], second], 0), 2)
        ext = jnp.concatenate([hi, hi, lo, jnp.zeros_like(hi)], 0)
        for i in range(dloc // 128):
            rows = slice(i * 128, (i + 1) * 128)
            a_ext[rows, :] = ext[:, rows].T.astype(BF16)

    got = bdot(lf[...], act[...], 1, 0)
    first = got[:BOTH] + got[BOTH : 2 * BOTH] + got[2 * BOTH :]
    hi, lo = pieces(jnp.concatenate([first, rpair[...]], 0), 2)
    b_ext[...] = jnp.concatenate([hi, lo, hi, jnp.zeros_like(hi)], 0).astype(BF16)
    scale = s_ref[0:1, 0:1]

    @pl.loop(0, dloc // step_m)
    def _(i):
        rows = pl.ds(pl.multiple_of(i * step_m, step_m), step_m)
        out[rows, :] = scale * bdot(gt[rows, :], act[...], 1, 0) + bdot(a_ext[rows, :], b_ext[...], 1, 0)


def stack_pairs(steps, curves):
    rows = ((0, HALF - steps.shape[0]), (0, 0))
    return jnp.concatenate([jnp.pad(steps, rows), jnp.pad(curves, rows)], 0)


def on_device(nrow, ncol, grad_out, activations, left_steps, left_curves, right_steps, right_curves):
    pairs = left_steps.shape[0]
    tok_c, dloc = grad_out.shape
    tok_r, floc = activations.shape
    tokens = tok_c * ncol
    lpair = stack_pairs(left_steps, left_curves)
    rpair = stack_pairs(right_steps, right_curves)
    aligned = tok_c % 128 == 0
    cuts = max(n for n in (1, 2, 4) if tok_r % (2 * n * 16) == 0)
    wide_c, wide_r = -(-tok_c // 128) * 128, -(-tok_r // 128) * 128
    ls, rs = stages(nrow), stages(ncol)
    hops_y = max(nrow // 4, 1)
    dma = pltpu.SemaphoreType.DMA
    vmem, anyw = pl.BlockSpec(memory_space=pltpu.VMEM), pl.BlockSpec(memory_space=pl.ANY)
    gt_shape = (dloc, tokens) if aligned else (ncol, dloc, tok_c)
    act_full, gt, lf, rf, x2, s = pl.pallas_call(
        functools.partial(gather_kernel, nrow, ncol, pairs, aligned, cuts, 0.12),
        out_shape=[
            jax.ShapeDtypeStruct((tokens, floc), BF16),
            jax.ShapeDtypeStruct(gt_shape, BF16),
            jax.ShapeDtypeStruct((3 * BOTH, tokens), BF16),
            jax.ShapeDtypeStruct((3 * BOTH, tokens), BF16),
            jax.ShapeDtypeStruct((BOTH, dloc), F32),
            jax.ShapeDtypeStruct((8, 128), F32),
        ],
        in_specs=[anyw, vmem, vmem, vmem],
        out_specs=[anyw, anyw, vmem, vmem, vmem, vmem],
        scratch_shapes=[
            pltpu.VMEM((dloc, tok_c), BF16),
            pltpu.VMEM((tok_r, floc), BF16),
            pltpu.VMEM((BOTH, wide_c + 128), F32),
            pltpu.VMEM((BOTH, wide_r + 128), F32),
            pltpu.VMEM((ls, BOTH, wide_c + 128), F32),
            pltpu.VMEM((rs, BOTH, wide_r + 128), F32),
            pltpu.VMEM((ls + 1, BOTH, wide_c + 128), F32),
            pltpu.VMEM((rs + 1, BOTH, wide_r + 128), F32),
            pltpu.VMEM((ncol, BOTH, wide_c), F32),
            pltpu.VMEM((nrow, BOTH, wide_r), F32),
            pltpu.VMEM((BOTH, tokens), F32),
            pltpu.VMEM((BOTH, tokens), F32),
            dma((5,)),
            dma((ncol // 2, 2)), dma((ncol // 2, 2)), dma((ncol // 2, 2)), dma((ncol // 2, 2)),
            dma((2, hops_y, 2 * cuts)), dma((2, hops_y, 2 * cuts)),
            dma((2, hops_y, 2 * cuts)), dma((2, hops_y, 2 * cuts)),
            dma((ls,)), dma((ls,)), dma((rs,)), dma((rs,)),
            dma((ncol,)), dma((ncol,)), dma((nrow,)), dma((nrow,)),
        ],
        compiler_params=pltpu.CompilerParams(
            collective_id=0, has_side_effects=True, vmem_limit_bytes=40 * 2**20),
        name="gather",
    )(activations, grad_out, lpair, rpair)
    if not aligned:
        gt = jnp.transpose(gt, (1, 0, 2)).reshape(dloc, tokens)
    step_n = max(n for n in (128, 256, 512) if floc % n == 0)
    step_m = min(512, dloc)

    def whole(shape):
        return pl.BlockSpec(shape, lambda j: (0, 0), pipeline_mode=pl.Buffered(1))

    return pl.pallas_call(
        functools.partial(apply_kernel, step_m),
        grid=(floc // step_n,),
        out_shape=jax.ShapeDtypeStruct((dloc, floc), F32),
        in_specs=[
            whole((8, 128)),
            whole((dloc, tokens)),
            pl.BlockSpec((tokens, step_n), lambda j: (0, j)),
            whole((3 * BOTH, tokens)),
            whole((3 * BOTH, tokens)),
            whole((BOTH, dloc)),
            whole((BOTH, dloc)),
            pl.BlockSpec((BOTH, step_n), lambda j: (0, j)),
        ],
        out_specs=pl.BlockSpec((dloc, step_n), lambda j: (0, j)),
        scratch_shapes=[pltpu.VMEM((dloc, 8 * BOTH), BF16), pltpu.VMEM((8 * BOTH, step_n), BF16)],
        compiler_params=pltpu.CompilerParams(vmem_limit_bytes=48 * 2**20),
        cost_estimate=pl.CostEstimate(
            flops=2 * dloc * floc * tokens, bytes_accessed=4 * dloc * floc, transcendentals=0),
        name="apply",
    )(s, gt, act_full, lf, rf, x2, lpair, rpair)


def solution(mesh):
    in_specs = (
        P("col", "row"),
        P("row", "col"),
        P(None, "row"),
        P(None, "row"),
        P(None, "col"),
        P(None, "col"),
    )
    out_specs = P("row", "col")
    body = functools.partial(on_device, mesh.shape["row"], mesh.shape["col"])
    return jax.shard_map(body, mesh=mesh, in_specs=in_specs, out_specs=out_specs, check_vma=False)
```

```python
import functools
import jax
import jax.numpy as jnp
from jax import lax
from jax.experimental import pallas as pl
from jax.experimental.pallas import tpu as pltpu
from jax.sharding import PartitionSpec as P

HIGH = lax.Precision.HIGHEST
MESH = pl.DeviceIdType.MESH
F32, BF16 = jnp.float32, jnp.bfloat16
HALF = 16
BOTH = 2 * HALF


def dot(a, b, ca, cb):
    return lax.dot_general(a, b, (((ca,), (cb,)), ((), ())), precision=HIGH, preferred_element_type=F32)


def bdot(a, b, ca, cb):
    return lax.dot_general(a, b, (((ca,), (cb,)), ((), ())), preferred_element_type=F32)


def pieces(x, count):
    out = []
    for _ in range(count):
        top = x.astype(BF16).astype(F32)
        out.append(top)
        x = x - top
    return out


def times_pieces(x, mat):
    rows = x.shape[0]
    got = bdot(jnp.concatenate(pieces(x, 3), 0).astype(BF16), mat, 1, 1)
    return got[:rows] + got[rows : 2 * rows] + got[2 * rows :]


def compact(prod, pairs):
    sub = lax.broadcasted_iota(jnp.int32, (HALF, HALF), 0)
    lane = lax.broadcasted_iota(jnp.int32, (HALF, HALF), 1)
    sy, yy = prod[:HALF], prod[HALF:]

    def pick(x, mask, axes):
        x = jnp.where(mask, x, 0.0)
        for axis in axes:
            x = jnp.sum(x, axis=axis, keepdims=True)
        return x

    last = (sub == pairs - 1) & (lane == pairs - 1)
    scaling = pick(sy, last, (0, 1)) / pick(yy, last, (0, 1))
    upper = jnp.where(sub <= lane, sy, 0.0)
    inv = jnp.where((sub == lane) & (sub < pairs), 1.0, 0.0)
    for j in reversed(range(pairs)):
        column = pick(upper, lane == j, (1,))
        row = pick(inv, sub == j, (0,)) / pick(upper, (sub == j) & (lane == j), (0, 1))
        inv = jnp.where(sub == j, row, jnp.where(sub < j, inv - column * row, inv))
    middle = jnp.where(sub == lane, sy, 0.0) + scaling * yy
    return scaling, inv, middle


def apply_terms(terms, x):
    scaling, inv, middle = terms
    weighted = dot(inv, x[:HALF], 1, 0)
    coeffs = dot(inv, dot(middle, weighted, 1, 0) - scaling * x[HALF:], 0, 0)
    return jnp.concatenate([coeffs, -scaling * weighted], 0)


def stages(n):
    return n.bit_length() - 1


def gather_kernel(
    nrow, ncol, pairs, aligned, cuts, fine, spread,
    act, go, lpair, rpair,
    act_full, gt_full, lf_out, rf_out, x2_out, s_out,
    gt, act_v, l_msg, r_msg, l_in, r_in, l_sum, r_sum, l_all, r_all, l_cat, r_cat,
    local_sem, own_s, own_r, cw_s, cw_r, cc_s, cc_r, y_s, y_r, sib_s, sib_r,
    l1_s, l1_r, r1_s, r1_r, l2_s, l2_r, r2_s, r2_r,
):
    r, c = lax.axis_index("row"), lax.axis_index("col")
    tok_r, tok_c, dloc = act.shape[0], go.shape[0], go.shape[1]
    ny = nrow // 2
    y, core = r // 2, r % 2
    nz = ncol // 2

    def dev(row, col):
        return {"row": row, "col": col}

    barrier = pltpu.get_barrier_semaphore()
    for d in range(1, nrow):
        pl.semaphore_signal(barrier, inc=1, device_id=dev((r + d) % nrow, c), device_id_type=MESH)
    for d in range(1, ncol):
        pl.semaphore_signal(barrier, inc=1, device_id=dev(r, (c + d) % ncol), device_id_type=MESH)
    pl.semaphore_wait(barrier, nrow + ncol - 2)

    pending = []

    def remote(src, dst, send, recv, row, col):
        copy = pltpu.make_async_remote_copy(
            src_ref=src, dst_ref=dst, send_sem=send, recv_sem=recv,
            device_id=dev(row, col), device_id_type=MESH)
        copy.start()
        pending.append(copy)
        return copy

    def local(src, dst, sem):
        copy = pltpu.make_async_copy(src, dst, sem)
        copy.start()
        return copy

    step_a = tok_r // (2 * cuts)

    def act_at(row, part):
        start = row * tok_r + part * step_a
        return act_full.at[pl.ds(pl.multiple_of(start, 16), step_a), :]

    def y_parts(k, way):
        full = ny // 2 - 1
        mine = range(way * cuts, (way + 1) * cuts)
        other = range((1 - way) * cuts, (2 - way) * cuts)
        return list(mine) + (list(other) if k < full else [])

    def y_send(k, way, part):
        sign = 1 - 2 * way
        origin = ((y - sign * k + ny) % ny) * 2 + core
        target = ((y + sign + ny) % ny) * 2 + core
        src = act.at[pl.ds(part * step_a, step_a), :] if k == 0 else act_at(origin, part)
        idx = (way, k, part)
        remote(src, act_at(origin, part), y_s.at[idx], y_r.at[idx], target, c)

    def y_wait(k, way, part):
        sign = 1 - 2 * way
        origin = ((y - sign * (k + 1) + 2 * ny) % ny) * 2 + core
        piece = act_at(origin, part)
        idx = (way, k, part)
        pltpu.make_async_remote_copy(
            src_ref=piece, dst_ref=piece, send_sem=y_s.at[idx], recv_sem=y_r.at[idx],
            device_id=dev(r, c), device_id_type=MESH).wait_recv()
        remote(piece, piece, sib_s.at[idx], sib_r.at[idx], y * 2 + 1 - core, c)
        if k + 1 < max(ny // 2, 1) and part in y_parts(k + 1, way):
            y_send(k + 1, way, part)

    def y_first(i):
        for way in range(2):
            y_send(0, way, y_parts(0, way)[i])

    own_act = act_full.at[pl.ds(pl.multiple_of(r * tok_r, 16), tok_r), :]
    to_v = local(act, act_v, local_sem.at[0])

    def own_sibling(part):
        src = act.at[pl.ds(part * step_a, step_a), :]
        remote(src, act_at(r, part), own_s.at[part], own_r.at[part], y * 2 + 1 - core, c)

    for i in range(dloc // 128):
        rows = slice(i * 128, (i + 1) * 128)
        gt[rows, :] = go[:, rows].astype(F32).T.astype(BF16)
    half = dloc // (2 * fine)
    zc, xc = c // 2, c % 2
    pos = (1 - xc) * zc + xc * (ncol - 1 - zc)

    def col_of(p):
        x = p // nz
        return ((1 - x) * p + x * (ncol - 1 - p)) * 2 + x

    def gt_at(col, h):
        if aligned:
            return gt_full.at[pl.ds(h * half, half), pl.ds(pl.multiple_of(col * tok_c, 128), tok_c)]
        return gt_full.at[col, pl.ds(h * half, half), :]

    def ring_halves(k, way):
        groups = [list(range(way * fine, (way + 1) * fine))]
        if k < ncol // 2 - 1:
            groups.append(list(range((1 - way) * fine, (2 - way) * fine)))
        return sum(groups, [])

    def ring_send(k, way, h):
        sign = 1 - 2 * way
        origin = col_of((pos - sign * k + ncol) % ncol)
        target = col_of((pos + sign + ncol) % ncol)
        src = gt.at[pl.ds(h * half, half), :] if k == 0 else gt_at(origin, h)
        send, recv = (cc_s, cc_r) if way else (cw_s, cw_r)
        remote(src, gt_at(origin, h), send.at[k, h], recv.at[k, h], r, target)

    def ring_wait(k, way, h):
        sign = 1 - 2 * way
        origin = col_of((pos - sign * (k + 1) + ncol) % ncol)
        piece = gt_at(origin, h)
        send, recv = (cc_s, cc_r) if way else (cw_s, cw_r)
        pltpu.make_async_remote_copy(
            src_ref=piece, dst_ref=piece, send_sem=send.at[k, h], recv_sem=recv.at[k, h],
            device_id=dev(r, c), device_id_type=MESH).wait_recv()
        if k + 1 < ncol // 2 and h in ring_halves(k + 1, way):
            ring_send(k + 1, way, h)

    for i in range(2 * fine):
        for way in range(2):
            ring_send(0, way, ring_halves(0, way)[i])
        if i < 2:
            y_first(i)
    if aligned:
        own_gt = gt_full.at[:, pl.ds(pl.multiple_of(c * tok_c, 128), tok_c)]
    else:
        own_gt = gt_full.at[c]
    keep_gt = local(gt, own_gt, local_sem.at[2])

    def first_part():
        lanes_l, lanes_r = l_msg.shape[1] - 128, r_msg.shape[1] - 128
        l_msg[...] = jnp.zeros_like(l_msg)
        l_msg[:, :tok_c] = times_pieces(lpair[...], go[...])
        l_msg[:, lanes_l : lanes_l + HALF] = dot(lpair[...], lpair[HALF:, :], 1, 1)
        to_v.wait()
        r_msg[...] = jnp.zeros_like(r_msg)
        r_msg[:, :tok_r] = times_pieces(rpair[...], act_v[...])
        r_msg[:, lanes_r : lanes_r + HALF] = dot(rpair[...], rpair[HALF:, :], 1, 1)
        l_sum[0] = l_msg[...]
        r_sum[0] = r_msg[...]

    def partner(i, s):
        return i + (1 - 2 * ((i // 2**s) % 2)) * 2**s

    def sum_start(s):
        if s < stages(nrow):
            remote(l_sum.at[s], l_in.at[s], l1_s.at[s], l1_r.at[s], partner(r, s), c)
        if s < stages(ncol):
            remote(r_sum.at[s], r_in.at[s], r1_s.at[s], r1_r.at[s], r, partner(c, s))

    def arrived(ref, send, recv):
        pltpu.make_async_remote_copy(
            src_ref=ref, dst_ref=ref, send_sem=send, recv_sem=recv,
            device_id=dev(r, c), device_id_type=MESH).wait_recv()

    def sum_end(s):
        if s < stages(nrow):
            arrived(l_in.at[s], l1_s.at[s], l1_r.at[s])
            l_sum[s + 1] = l_sum[s] + l_in[s]
        if s < stages(ncol):
            arrived(r_in.at[s], r1_s.at[s], r1_r.at[s])
            r_sum[s + 1] = r_sum[s] + r_in[s]

    ls, rs = stages(nrow), stages(ncol)

    def spread_sums():
        l_own = l_sum.at[ls, :, pl.ds(0, l_all.shape[2])]
        r_own = r_sum.at[rs, :, pl.ds(0, r_all.shape[2])]
        for d in range(1, ncol):
            remote(l_own, l_all.at[c], l2_s.at[d], l2_r.at[d], r, (c + d) % ncol)
        for d in range(1, nrow):
            remote(r_own, r_all.at[r], r2_s.at[d], r2_r.at[d], (r + d) % nrow, c)
        l_all[c] = l_sum[ls, :, : l_all.shape[2]]
        r_all[r] = r_sum[rs, :, : r_all.shape[2]]

    def last_part():
        for d in range(1, ncol):
            arrived(l_all.at[(c + ncol - d) % ncol], l2_s.at[d], l2_r.at[d])
        for d in range(1, nrow):
            arrived(r_all.at[(r + nrow - d) % nrow], r2_s.at[d], r2_r.at[d])
        for i in range(ncol):
            l_cat[:, i * tok_c : (i + 1) * tok_c] = l_all[i, :, :tok_c]
        for i in range(nrow):
            r_cat[:, i * tok_r : (i + 1) * tok_r] = r_all[i, :, :tok_r]
        left = compact(l_sum[ls, :, l_all.shape[2] : l_all.shape[2] + HALF], pairs)
        right = compact(r_sum[rs, :, r_all.shape[2] : r_all.shape[2] + HALF], pairs)
        lf = right[0] * apply_terms(left, l_cat[...])
        rf = left[0] * apply_terms(right, r_cat[...])
        for i, piece in enumerate(pieces(lf, 3)):
            lf_out[i * BOTH : (i + 1) * BOTH, :] = piece.astype(BF16)
        for i, piece in enumerate(pieces(rf, 3)):
            rf_out[i * BOTH : (i + 1) * BOTH, :] = piece.astype(BF16)
        cross = dot(l_cat[...], r_cat[...], 1, 1)
        x2_out[...] = apply_terms(right, dot(cross, apply_terms(left, lpair[...]), 0, 0))
        s_out[...] = jnp.broadcast_to(left[0] * right[0], s_out.shape)

    todo = []
    ring_total = (ncol - 1) * fine
    done = 0
    for k in range(ncol // 2):
        for i in range(len(ring_halves(k, 0))):
            done += 1
            for way in range(2):
                h = ring_halves(k, way)[i]
                todo.append((done / ring_total, functools.partial(ring_wait, k, way, h)))
    y_count = sum(len(y_parts(k, 0)) for k in range(max(ny // 2, 1)))
    done = 0
    for k in range(max(ny // 2, 1)):
        for i in range(len(y_parts(k, 0))):
            if k == 0 and i >= 2:
                todo.append(((i - 1.5) / y_count, functools.partial(y_first, i)))
            done += 1
            for way in range(2):
                todo.append((done / y_count + 0.2, functools.partial(y_wait, k, way, y_parts(k, way)[i])))
    for part in range(2 * cuts):
        todo.append((0.1 + 0.8 * part / (2 * cuts), functools.partial(own_sibling, part)))
    keep_act = pltpu.make_async_copy(act, own_act, local_sem.at[1])
    todo.append((0.35, keep_act.start))
    small = [first_part, functools.partial(sum_start, 0)]
    for s in range(max(ls, rs)):
        small.append((lambda s: lambda: (sum_end(s), sum_start(s + 1)))(s))
    small += [spread_sums, last_part]
    for i, f in enumerate(small[:-2]):
        todo.append((max(0, i - 1) * spread + 0.001, f))
    late = max(ls, rs) * spread + 0.002
    todo += [(late, small[-2]), (late + 1.5 * spread, small[-1])]
    todo.sort(key=lambda item: item[0])
    for _, f in todo:
        f()
    for part in range(2 * cuts):
        arrived(act_at(y * 2 + 1 - core, part), own_s.at[part], own_r.at[part])
    for k in range(max(ny // 2, 1)):
        for way in range(2):
            sign = 1 - 2 * way
            origin = ((y - sign * (k + 1) + 2 * ny) % ny) * 2 + 1 - core
            for part in y_parts(k, way):
                arrived(act_at(origin, part), sib_s.at[way, k, part], sib_r.at[way, k, part])
    keep_act.wait()
    keep_gt.wait()
    for copy in pending:
        copy.wait_send()


def apply_kernel(step_m, s_ref, gt, act, lf, rf, x2, lpair, rpair, out, a_ext, b_ext):
    wide = 2 * BOTH
    dloc = gt.shape[0]

    @pl.when(pl.program_id(0) == 0)
    def _():
        got = bdot(rf[...], gt[...], 1, 1)
        second = got[:BOTH] + got[BOTH : 2 * BOTH] + got[2 * BOTH :] + x2[...]
        hi, lo = pieces(jnp.concatenate([lpair[...], second], 0), 2)
        ext = jnp.concatenate([hi, hi, lo, jnp.zeros_like(hi)], 0)
        for i in range(dloc // 128):
            rows = slice(i * 128, (i + 1) * 128)
            a_ext[rows, :] = ext[:, rows].T.astype(BF16)

    got = bdot(lf[...], act[...], 1, 0)
    first = got[:BOTH] + got[BOTH : 2 * BOTH] + got[2 * BOTH :]
    hi, lo = pieces(jnp.concatenate([first, rpair[...]], 0), 2)
    b_ext[...] = jnp.concatenate([hi, lo, hi, jnp.zeros_like(hi)], 0).astype(BF16)
    scale = s_ref[0:1, 0:1]

    @pl.loop(0, dloc // step_m)
    def _(i):
        rows = pl.ds(pl.multiple_of(i * step_m, step_m), step_m)
        out[rows, :] = scale * bdot(gt[rows, :], act[...], 1, 0) + bdot(a_ext[rows, :], b_ext[...], 1, 0)


def stack_pairs(steps, curves):
    rows = ((0, HALF - steps.shape[0]), (0, 0))
    return jnp.concatenate([jnp.pad(steps, rows), jnp.pad(curves, rows)], 0)


def on_device(nrow, ncol, grad_out, activations, left_steps, left_curves, right_steps, right_curves):
    pairs = left_steps.shape[0]
    tok_c, dloc = grad_out.shape
    tok_r, floc = activations.shape
    tokens = tok_c * ncol
    lpair = stack_pairs(left_steps, left_curves)
    rpair = stack_pairs(right_steps, right_curves)
    aligned = tok_c % 128 == 0
    cuts = max(n for n in (1, 2, 4, 8) if tok_r % (2 * n * 16) == 0)
    fine = max(n for n in (1, 2) if dloc % (2 * n * 16) == 0)
    wide_c, wide_r = -(-tok_c // 128) * 128, -(-tok_r // 128) * 128
    ls, rs = stages(nrow), stages(ncol)
    hops_y = max(nrow // 4, 1)
    dma = pltpu.SemaphoreType.DMA
    vmem, anyw = pl.BlockSpec(memory_space=pltpu.VMEM), pl.BlockSpec(memory_space=pl.ANY)
    gt_shape = (dloc, tokens) if aligned else (ncol, dloc, tok_c)
    act_full, gt, lf, rf, x2, s = pl.pallas_call(
        functools.partial(gather_kernel, nrow, ncol, pairs, aligned, cuts, fine, 0.15),
        out_shape=[
            jax.ShapeDtypeStruct((tokens, floc), BF16),
            jax.ShapeDtypeStruct(gt_shape, BF16),
            jax.ShapeDtypeStruct((3 * BOTH, tokens), BF16),
            jax.ShapeDtypeStruct((3 * BOTH, tokens), BF16),
            jax.ShapeDtypeStruct((BOTH, dloc), F32),
            jax.ShapeDtypeStruct((8, 128), F32),
        ],
        in_specs=[anyw, vmem, vmem, vmem],
        out_specs=[anyw, anyw, vmem, vmem, vmem, vmem],
        scratch_shapes=[
            pltpu.VMEM((dloc, tok_c), BF16),
            pltpu.VMEM((tok_r, floc), BF16),
            pltpu.VMEM((BOTH, wide_c + 128), F32),
            pltpu.VMEM((BOTH, wide_r + 128), F32),
            pltpu.VMEM((ls, BOTH, wide_c + 128), F32),
            pltpu.VMEM((rs, BOTH, wide_r + 128), F32),
            pltpu.VMEM((ls + 1, BOTH, wide_c + 128), F32),
            pltpu.VMEM((rs + 1, BOTH, wide_r + 128), F32),
            pltpu.VMEM((ncol, BOTH, wide_c), F32),
            pltpu.VMEM((nrow, BOTH, wide_r), F32),
            pltpu.VMEM((BOTH, tokens), F32),
            pltpu.VMEM((BOTH, tokens), F32),
            dma((3,)),
            dma((2 * cuts,)), dma((2 * cuts,)),
            dma((ncol // 2, 2 * fine)), dma((ncol // 2, 2 * fine)), dma((ncol // 2, 2 * fine)), dma((ncol // 2, 2 * fine)),
            dma((2, hops_y, 2 * cuts)), dma((2, hops_y, 2 * cuts)),
            dma((2, hops_y, 2 * cuts)), dma((2, hops_y, 2 * cuts)),
            dma((ls,)), dma((ls,)), dma((rs,)), dma((rs,)),
            dma((ncol,)), dma((ncol,)), dma((nrow,)), dma((nrow,)),
        ],
        compiler_params=pltpu.CompilerParams(
            collective_id=0, has_side_effects=True, vmem_limit_bytes=40 * 2**20),
        name="gather",
    )(activations, grad_out, lpair, rpair)
    if not aligned:
        gt = jnp.transpose(gt, (1, 0, 2)).reshape(dloc, tokens)
    step_n = max(n for n in (128, 256, 512) if floc % n == 0)
    step_m = min(512, dloc)

    def whole(shape):
        return pl.BlockSpec(shape, lambda j: (0, 0), pipeline_mode=pl.Buffered(1))

    return pl.pallas_call(
        functools.partial(apply_kernel, step_m),
        grid=(floc // step_n,),
        out_shape=jax.ShapeDtypeStruct((dloc, floc), F32),
        in_specs=[
            whole((8, 128)),
            whole((dloc, tokens)),
            pl.BlockSpec((tokens, step_n), lambda j: (0, j)),
            whole((3 * BOTH, tokens)),
            whole((3 * BOTH, tokens)),
            whole((BOTH, dloc)),
            whole((BOTH, dloc)),
            pl.BlockSpec((BOTH, step_n), lambda j: (0, j)),
        ],
        out_specs=pl.BlockSpec((dloc, step_n), lambda j: (0, j)),
        scratch_shapes=[pltpu.VMEM((dloc, 8 * BOTH), BF16), pltpu.VMEM((8 * BOTH, step_n), BF16)],
        compiler_params=pltpu.CompilerParams(vmem_limit_bytes=48 * 2**20),
        cost_estimate=pl.CostEstimate(
            flops=2 * dloc * floc * tokens, bytes_accessed=4 * dloc * floc, transcendentals=0),
        name="apply",
    )(s, gt, act_full, lf, rf, x2, lpair, rpair)


def solution(mesh):
    in_specs = (
        P("col", "row"),
        P("row", "col"),
        P(None, "row"),
        P(None, "row"),
        P(None, "col"),
        P(None, "col"),
    )
    out_specs = P("row", "col")
    body = functools.partial(on_device, mesh.shape["row"], mesh.shape["col"])
    return jax.shard_map(body, mesh=mesh, in_specs=in_specs, out_specs=out_specs, check_vma=False)
```

```python
import functools
import jax
import jax.numpy as jnp
from jax import lax
from jax.experimental import pallas as pl
from jax.experimental.pallas import tpu as pltpu
from jax.sharding import PartitionSpec as P

HIGH = lax.Precision.HIGHEST
MESH = pl.DeviceIdType.MESH
F32, BF16 = jnp.float32, jnp.bfloat16
HALF = 16
BOTH = 2 * HALF


def dot(a, b, ca, cb):
    return lax.dot_general(a, b, (((ca,), (cb,)), ((), ())), precision=HIGH, preferred_element_type=F32)


def bdot(a, b, ca, cb):
    return lax.dot_general(a, b, (((ca,), (cb,)), ((), ())), preferred_element_type=F32)


def pieces(x, count):
    out = []
    for _ in range(count):
        top = x.astype(BF16).astype(F32)
        out.append(top)
        x = x - top
    return out


def times_pieces(x, mat):
    rows = x.shape[0]
    got = bdot(jnp.concatenate(pieces(x, 3), 0).astype(BF16), mat, 1, 1)
    return got[:rows] + got[rows : 2 * rows] + got[2 * rows :]


def compact(prod, pairs):
    sub = lax.broadcasted_iota(jnp.int32, (HALF, HALF), 0)
    lane = lax.broadcasted_iota(jnp.int32, (HALF, HALF), 1)
    sy, yy = prod[:HALF], prod[HALF:]

    def pick(x, mask, axes):
        x = jnp.where(mask, x, 0.0)
        for axis in axes:
            x = jnp.sum(x, axis=axis, keepdims=True)
        return x

    last = (sub == pairs - 1) & (lane == pairs - 1)
    scaling = pick(sy, last, (0, 1)) / pick(yy, last, (0, 1))
    upper = jnp.where(sub <= lane, sy, 0.0)
    inv = jnp.where((sub == lane) & (sub < pairs), 1.0, 0.0)
    for j in reversed(range(pairs)):
        column = pick(upper, lane == j, (1,))
        row = pick(inv, sub == j, (0,)) / pick(upper, (sub == j) & (lane == j), (0, 1))
        inv = jnp.where(sub == j, row, jnp.where(sub < j, inv - column * row, inv))
    middle = jnp.where(sub == lane, sy, 0.0) + scaling * yy
    return scaling, inv, middle


def apply_terms(terms, x):
    scaling, inv, middle = terms
    weighted = dot(inv, x[:HALF], 1, 0)
    coeffs = dot(inv, dot(middle, weighted, 1, 0) - scaling * x[HALF:], 0, 0)
    return jnp.concatenate([coeffs, -scaling * weighted], 0)


def stages(n):
    return n.bit_length() - 1


def gather_kernel(
    nrow, ncol, pairs, aligned, cuts, fine, spread,
    act, go_any, lpair, rpair,
    act_full, gt_full, lf_out, rf_out, x2_out, s_out,
    go, gt, act_v, l_msg, r_msg, l_in, r_in, l_sum, r_sum, l_all, r_all, l_cat, r_cat,
    go_sem, local_sem, own_s, own_r, cw_s, cw_r, cc_s, cc_r, y_s, y_r, sib_s, sib_r,
    l1_s, l1_r, r1_s, r1_r, l2_s, l2_r, r2_s, r2_r,
):
    r, c = lax.axis_index("row"), lax.axis_index("col")
    tok_r, tok_c, dloc = act.shape[0], go.shape[0], go.shape[1]
    ny = nrow // 2
    y, core = r // 2, r % 2
    nz = ncol // 2

    def dev(row, col):
        return {"row": row, "col": col}

    to_go = pltpu.make_async_copy(go_any, go, go_sem)
    to_go.start()
    barrier = pltpu.get_barrier_semaphore()
    for d in range(1, nrow):
        pl.semaphore_signal(barrier, inc=1, device_id=dev((r + d) % nrow, c), device_id_type=MESH)
    for d in range(1, ncol):
        pl.semaphore_signal(barrier, inc=1, device_id=dev(r, (c + d) % ncol), device_id_type=MESH)
    pl.semaphore_wait(barrier, nrow + ncol - 2)

    pending = []

    def remote(src, dst, send, recv, row, col):
        copy = pltpu.make_async_remote_copy(
            src_ref=src, dst_ref=dst, send_sem=send, recv_sem=recv,
            device_id=dev(row, col), device_id_type=MESH)
        copy.start()
        pending.append(copy)
        return copy

    def local(src, dst, sem):
        copy = pltpu.make_async_copy(src, dst, sem)
        copy.start()
        return copy

    step_a = tok_r // (2 * cuts)

    def act_at(row, part):
        start = row * tok_r + part * step_a
        return act_full.at[pl.ds(pl.multiple_of(start, 16), step_a), :]

    def y_parts(k, way):
        full = ny // 2 - 1
        mine = range(way * cuts, (way + 1) * cuts)
        other = range((1 - way) * cuts, (2 - way) * cuts)
        return list(mine) + (list(other) if k < full else [])

    def y_send(k, way, part):
        sign = 1 - 2 * way
        origin = ((y - sign * k + ny) % ny) * 2 + core
        target = ((y + sign + ny) % ny) * 2 + core
        src = act.at[pl.ds(part * step_a, step_a), :] if k == 0 else act_at(origin, part)
        idx = (way, k, part)
        remote(src, act_at(origin, part), y_s.at[idx], y_r.at[idx], target, c)

    def y_wait(k, way, part):
        sign = 1 - 2 * way
        origin = ((y - sign * (k + 1) + 2 * ny) % ny) * 2 + core
        piece = act_at(origin, part)
        idx = (way, k, part)
        pltpu.make_async_remote_copy(
            src_ref=piece, dst_ref=piece, send_sem=y_s.at[idx], recv_sem=y_r.at[idx],
            device_id=dev(r, c), device_id_type=MESH).wait_recv()
        remote(piece, piece, sib_s.at[idx], sib_r.at[idx], y * 2 + 1 - core, c)
        if k + 1 < max(ny // 2, 1) and part in y_parts(k + 1, way):
            y_send(k + 1, way, part)

    def y_first(i):
        for way in range(2):
            y_send(0, way, y_parts(0, way)[i])

    own_act = act_full.at[pl.ds(pl.multiple_of(r * tok_r, 16), tok_r), :]
    to_v = local(act, act_v, local_sem.at[0])

    def own_sibling(part):
        src = act.at[pl.ds(part * step_a, step_a), :]
        remote(src, act_at(r, part), own_s.at[part], own_r.at[part], y * 2 + 1 - core, c)

    to_go.wait()
    for i in range(dloc // 128):
        rows = slice(i * 128, (i + 1) * 128)
        gt[rows, :] = go[:, rows].astype(F32).T.astype(BF16)
    half = dloc // (2 * fine)
    zc, xc = c // 2, c % 2
    pos = (1 - xc) * zc + xc * (ncol - 1 - zc)

    def col_of(p):
        x = p // nz
        return ((1 - x) * p + x * (ncol - 1 - p)) * 2 + x

    def gt_at(col, h):
        if aligned:
            return gt_full.at[pl.ds(h * half, half), pl.ds(pl.multiple_of(col * tok_c, 128), tok_c)]
        return gt_full.at[col, pl.ds(h * half, half), :]

    def ring_halves(k, way):
        groups = [list(range(way * fine, (way + 1) * fine))]
        if k < ncol // 2 - 1:
            groups.append(list(range((1 - way) * fine, (2 - way) * fine)))
        return sum(groups, [])

    def ring_send(k, way, h):
        sign = 1 - 2 * way
        origin = col_of((pos - sign * k + ncol) % ncol)
        target = col_of((pos + sign + ncol) % ncol)
        src = gt.at[pl.ds(h * half, half), :] if k == 0 else gt_at(origin, h)
        send, recv = (cc_s, cc_r) if way else (cw_s, cw_r)
        remote(src, gt_at(origin, h), send.at[k, h], recv.at[k, h], r, target)

    def ring_wait(k, way, h):
        sign = 1 - 2 * way
        origin = col_of((pos - sign * (k + 1) + ncol) % ncol)
        piece = gt_at(origin, h)
        send, recv = (cc_s, cc_r) if way else (cw_s, cw_r)
        pltpu.make_async_remote_copy(
            src_ref=piece, dst_ref=piece, send_sem=send.at[k, h], recv_sem=recv.at[k, h],
            device_id=dev(r, c), device_id_type=MESH).wait_recv()
        if k + 1 < ncol // 2 and h in ring_halves(k + 1, way):
            ring_send(k + 1, way, h)

    for i in range(2 * fine):
        for way in range(2):
            ring_send(0, way, ring_halves(0, way)[i])
        if i < 2:
            y_first(i)
    if aligned:
        own_gt = gt_full.at[:, pl.ds(pl.multiple_of(c * tok_c, 128), tok_c)]
    else:
        own_gt = gt_full.at[c]
    keep_gt = local(gt, own_gt, local_sem.at[2])

    def first_part():
        lanes_l, lanes_r = l_msg.shape[1] - 128, r_msg.shape[1] - 128
        l_msg[...] = jnp.zeros_like(l_msg)
        l_msg[:, :tok_c] = times_pieces(lpair[...], go[...])
        l_msg[:, lanes_l : lanes_l + HALF] = dot(lpair[...], lpair[HALF:, :], 1, 1)
        to_v.wait()
        r_msg[...] = jnp.zeros_like(r_msg)
        r_msg[:, :tok_r] = times_pieces(rpair[...], act_v[...])
        r_msg[:, lanes_r : lanes_r + HALF] = dot(rpair[...], rpair[HALF:, :], 1, 1)
        l_sum[0] = l_msg[...]
        r_sum[0] = r_msg[...]

    def partner(i, s):
        return i + (1 - 2 * ((i // 2**s) % 2)) * 2**s

    def sum_start(s):
        if s < stages(nrow):
            remote(l_sum.at[s], l_in.at[s], l1_s.at[s], l1_r.at[s], partner(r, s), c)
        if s < stages(ncol):
            remote(r_sum.at[s], r_in.at[s], r1_s.at[s], r1_r.at[s], r, partner(c, s))

    def arrived(ref, send, recv):
        pltpu.make_async_remote_copy(
            src_ref=ref, dst_ref=ref, send_sem=send, recv_sem=recv,
            device_id=dev(r, c), device_id_type=MESH).wait_recv()

    def sum_end(s):
        if s < stages(nrow):
            arrived(l_in.at[s], l1_s.at[s], l1_r.at[s])
            l_sum[s + 1] = l_sum[s] + l_in[s]
        if s < stages(ncol):
            arrived(r_in.at[s], r1_s.at[s], r1_r.at[s])
            r_sum[s + 1] = r_sum[s] + r_in[s]

    ls, rs = stages(nrow), stages(ncol)

    def spread_sums():
        l_own = l_sum.at[ls, :, pl.ds(0, l_all.shape[2])]
        r_own = r_sum.at[rs, :, pl.ds(0, r_all.shape[2])]
        for d in range(1, ncol):
            remote(l_own, l_all.at[c], l2_s.at[d], l2_r.at[d], r, (c + d) % ncol)
        for d in range(1, nrow):
            remote(r_own, r_all.at[r], r2_s.at[d], r2_r.at[d], (r + d) % nrow, c)
        l_all[c] = l_sum[ls, :, : l_all.shape[2]]
        r_all[r] = r_sum[rs, :, : r_all.shape[2]]

    def last_part():
        for d in range(1, ncol):
            arrived(l_all.at[(c + ncol - d) % ncol], l2_s.at[d], l2_r.at[d])
        for d in range(1, nrow):
            arrived(r_all.at[(r + nrow - d) % nrow], r2_s.at[d], r2_r.at[d])
        for i in range(ncol):
            l_cat[:, i * tok_c : (i + 1) * tok_c] = l_all[i, :, :tok_c]
        for i in range(nrow):
            r_cat[:, i * tok_r : (i + 1) * tok_r] = r_all[i, :, :tok_r]
        left = compact(l_sum[ls, :, l_all.shape[2] : l_all.shape[2] + HALF], pairs)
        right = compact(r_sum[rs, :, r_all.shape[2] : r_all.shape[2] + HALF], pairs)
        lf = right[0] * apply_terms(left, l_cat[...])
        rf = left[0] * apply_terms(right, r_cat[...])
        for i, piece in enumerate(pieces(lf, 2)):
            lf_out[i * BOTH : (i + 1) * BOTH, :] = piece.astype(BF16)
        for i, piece in enumerate(pieces(rf, 2)):
            rf_out[i * BOTH : (i + 1) * BOTH, :] = piece.astype(BF16)
        cross = dot(l_cat[...], r_cat[...], 1, 1)
        x2_out[...] = apply_terms(right, dot(cross, apply_terms(left, lpair[...]), 0, 0))
        s_out[...] = jnp.broadcast_to(left[0] * right[0], s_out.shape)

    todo = []
    ring_total = (ncol - 1) * fine
    done = 0
    for k in range(ncol // 2):
        for i in range(len(ring_halves(k, 0))):
            done += 1
            for way in range(2):
                h = ring_halves(k, way)[i]
                todo.append((done / ring_total, functools.partial(ring_wait, k, way, h)))
    y_count = sum(len(y_parts(k, 0)) for k in range(max(ny // 2, 1)))
    done = 0
    for k in range(max(ny // 2, 1)):
        for i in range(len(y_parts(k, 0))):
            if k == 0 and i >= 2:
                todo.append(((i - 1.5) / y_count, functools.partial(y_first, i)))
            done += 1
            for way in range(2):
                todo.append((done / y_count + 0.2, functools.partial(y_wait, k, way, y_parts(k, way)[i])))
    for part in range(2 * cuts):
        todo.append((0.1 + 0.8 * part / (2 * cuts), functools.partial(own_sibling, part)))
    keep_act = pltpu.make_async_copy(act, own_act, local_sem.at[1])
    todo.append((0.35, keep_act.start))
    small = [first_part, functools.partial(sum_start, 0)]
    for s in range(max(ls, rs)):
        small.append((lambda s: lambda: (sum_end(s), sum_start(s + 1)))(s))
    small += [spread_sums, last_part]
    for i, f in enumerate(small[:-2]):
        todo.append((max(0, i - 1) * spread + 0.001, f))
    late = max(ls, rs) * spread + 0.002
    todo += [(late, small[-2]), (late + 1.5 * spread, small[-1])]
    todo.sort(key=lambda item: item[0])
    for _, f in todo:
        f()
    for part in range(2 * cuts):
        arrived(act_at(y * 2 + 1 - core, part), own_s.at[part], own_r.at[part])
    for k in range(max(ny // 2, 1)):
        for way in range(2):
            sign = 1 - 2 * way
            origin = ((y - sign * (k + 1) + 2 * ny) % ny) * 2 + 1 - core
            for part in y_parts(k, way):
                arrived(act_at(origin, part), sib_s.at[way, k, part], sib_r.at[way, k, part])
    keep_act.wait()
    keep_gt.wait()
    for copy in pending:
        copy.wait_send()


def apply_kernel(step_m, s_ref, gt, act, lf, rf, x2, lpair, rpair, out, a_ext, b_ext):
    wide = 2 * BOTH
    dloc = gt.shape[0]

    @pl.when(pl.program_id(0) == 0)
    def _():
        got = bdot(rf[...], gt[...], 1, 1)
        second = got[:BOTH] + got[BOTH:] + x2[...]
        hi, lo = pieces(jnp.concatenate([lpair[...], second], 0), 2)
        ext = jnp.concatenate([hi, hi, lo, jnp.zeros_like(hi)], 0)
        for i in range(dloc // 128):
            rows = slice(i * 128, (i + 1) * 128)
            a_ext[rows, :] = ext[:, rows].T.astype(BF16)

    got = bdot(lf[...], act[...], 1, 0)
    first = got[:BOTH] + got[BOTH:]
    hi, lo = pieces(jnp.concatenate([first, rpair[...]], 0), 2)
    b_ext[...] = jnp.concatenate([hi, lo, hi, jnp.zeros_like(hi)], 0).astype(BF16)
    scale = s_ref[0:1, 0:1]

    @pl.loop(0, dloc // step_m)
    def _(i):
        rows = pl.ds(pl.multiple_of(i * step_m, step_m), step_m)
        out[rows, :] = scale * bdot(gt[rows, :], act[...], 1, 0) + bdot(a_ext[rows, :], b_ext[...], 1, 0)


def stack_pairs(steps, curves):
    rows = ((0, HALF - steps.shape[0]), (0, 0))
    return jnp.concatenate([jnp.pad(steps, rows), jnp.pad(curves, rows)], 0)


def on_device(nrow, ncol, grad_out, activations, left_steps, left_curves, right_steps, right_curves):
    pairs = left_steps.shape[0]
    tok_c, dloc = grad_out.shape
    tok_r, floc = activations.shape
    tokens = tok_c * ncol
    lpair = stack_pairs(left_steps, left_curves)
    rpair = stack_pairs(right_steps, right_curves)
    aligned = tok_c % 128 == 0
    cuts = max(n for n in (1, 2, 4, 8) if tok_r % (2 * n * 16) == 0)
    fine = max(n for n in (1, 2) if dloc % (2 * n * 16) == 0)
    wide_c, wide_r = -(-tok_c // 128) * 128, -(-tok_r // 128) * 128
    ls, rs = stages(nrow), stages(ncol)
    hops_y = max(nrow // 4, 1)
    dma = pltpu.SemaphoreType.DMA
    vmem, anyw = pl.BlockSpec(memory_space=pltpu.VMEM), pl.BlockSpec(memory_space=pl.ANY)
    gt_shape = (dloc, tokens) if aligned else (ncol, dloc, tok_c)
    act_full, gt, lf, rf, x2, s = pl.pallas_call(
        functools.partial(gather_kernel, nrow, ncol, pairs, aligned, cuts, fine, 0.15),
        out_shape=[
            jax.ShapeDtypeStruct((tokens, floc), BF16),
            jax.ShapeDtypeStruct(gt_shape, BF16),
            jax.ShapeDtypeStruct((2 * BOTH, tokens), BF16),
            jax.ShapeDtypeStruct((2 * BOTH, tokens), BF16),
            jax.ShapeDtypeStruct((BOTH, dloc), F32),
            jax.ShapeDtypeStruct((8, 128), F32),
        ],
        in_specs=[anyw, anyw, vmem, vmem],
        out_specs=[anyw, anyw, vmem, vmem, vmem, vmem],
        scratch_shapes=[
            pltpu.VMEM((tok_c, dloc), BF16),
            pltpu.VMEM((dloc, tok_c), BF16),
            pltpu.VMEM((tok_r, floc), BF16),
            pltpu.VMEM((BOTH, wide_c + 128), F32),
            pltpu.VMEM((BOTH, wide_r + 128), F32),
            pltpu.VMEM((ls, BOTH, wide_c + 128), F32),
            pltpu.VMEM((rs, BOTH, wide_r + 128), F32),
            pltpu.VMEM((ls + 1, BOTH, wide_c + 128), F32),
            pltpu.VMEM((rs + 1, BOTH, wide_r + 128), F32),
            pltpu.VMEM((ncol, BOTH, wide_c), F32),
            pltpu.VMEM((nrow, BOTH, wide_r), F32),
            pltpu.VMEM((BOTH, tokens), F32),
            pltpu.VMEM((BOTH, tokens), F32),
            dma(()), dma((3,)),
            dma((2 * cuts,)), dma((2 * cuts,)),
            dma((ncol // 2, 2 * fine)), dma((ncol // 2, 2 * fine)), dma((ncol // 2, 2 * fine)), dma((ncol // 2, 2 * fine)),
            dma((2, hops_y, 2 * cuts)), dma((2, hops_y, 2 * cuts)),
            dma((2, hops_y, 2 * cuts)), dma((2, hops_y, 2 * cuts)),
            dma((ls,)), dma((ls,)), dma((rs,)), dma((rs,)),
            dma((ncol,)), dma((ncol,)), dma((nrow,)), dma((nrow,)),
        ],
        compiler_params=pltpu.CompilerParams(
            collective_id=0, has_side_effects=True, vmem_limit_bytes=40 * 2**20),
        name="gather",
    )(activations, grad_out, lpair, rpair)
    if not aligned:
        gt = jnp.transpose(gt, (1, 0, 2)).reshape(dloc, tokens)
    step_n = max(n for n in (128, 256, 512) if floc % n == 0)
    step_m = min(1024, dloc)

    def whole(shape):
        return pl.BlockSpec(shape, lambda j: (0, 0), pipeline_mode=pl.Buffered(1))

    return pl.pallas_call(
        functools.partial(apply_kernel, step_m),
        grid=(floc // step_n,),
        out_shape=jax.ShapeDtypeStruct((dloc, floc), F32),
        in_specs=[
            whole((8, 128)),
            whole((dloc, tokens)),
            pl.BlockSpec((tokens, step_n), lambda j: (0, j)),
            whole((2 * BOTH, tokens)),
            whole((2 * BOTH, tokens)),
            whole((BOTH, dloc)),
            whole((BOTH, dloc)),
            pl.BlockSpec((BOTH, step_n), lambda j: (0, j)),
        ],
        out_specs=pl.BlockSpec((dloc, step_n), lambda j: (0, j)),
        scratch_shapes=[pltpu.VMEM((dloc, 8 * BOTH), BF16), pltpu.VMEM((8 * BOTH, step_n), BF16)],
        compiler_params=pltpu.CompilerParams(vmem_limit_bytes=48 * 2**20),
        cost_estimate=pl.CostEstimate(
            flops=2 * dloc * floc * tokens, bytes_accessed=4 * dloc * floc, transcendentals=0),
        name="apply",
    )(s, gt, act_full, lf, rf, x2, lpair, rpair)


def solution(mesh):
    in_specs = (
        P("col", "row"),
        P("row", "col"),
        P(None, "row"),
        P(None, "row"),
        P(None, "col"),
        P(None, "col"),
    )
    out_specs = P("row", "col")
    body = functools.partial(on_device, mesh.shape["row"], mesh.shape["col"])
    return jax.shard_map(body, mesh=mesh, in_specs=in_specs, out_specs=out_specs, check_vma=False)
```
